128 devices in a mesh: facet: 4 (over y), pix: 8 (over z, core), chan: 4 (over x).
Axes of the slice: x: 4, y: 4, z: 4, core: 2. Of those that a mesh axis runs over, the one named last changes fastest.
Arguments:
- facets: float32 [4, 24, 1024, 1024], P('facet', 'pix', None, 'chan'), may hold values from -600 to 600, as said below
- profiles: float32 [8, 1024], replicated, may hold values from 0.25 to 1
- profile_index: int32 [4, 24], P('facet', 'pix'), may hold values from 0 to 7
Outputs:
- summed_facets: float32 [4, 24, 1024, 1024], P('facet', 'pix', None, 'chan')
The draws below stay inside these ranges and needn't reach their ends.
Inputs may be any that keep to these rules, and one draw needn't show every extreme that they name: `facets`: real-valued image cubes whose pixels and channels have different scales.
All inputs are finite; a program needn't handle non-finite values.
Results may differ from the reference program's by a relative error of at most 0.0001.
Values sent between devices are 32-bit elements; how exact they have to be, the bound alone decides.
A program may use at most 64 MiB of HBM per device.

```python
import math
import jax
import jax.numpy as jnp
from jax import lax

CHANNELS = 1024
FCOLS = 1024
OV = 128
ITERS = 4
NPROF = 8
FACETS = 4
ROWS = 24


def draw_facets(key, part):
    key = jax.random.fold_in(key, 11)
    key_base, key_pixel, key_channel = jax.random.split(key, 3)
    shape = (FACETS, ROWS, FCOLS, CHANNELS)
    base = jnp.clip(jax.random.normal(key_base, shape, jnp.float32), -4.0, 4.0)
    upper = math.log(10.0)
    pixel_scale = jnp.exp(jax.random.uniform(key_pixel, (FACETS, ROWS, FCOLS, 1), jnp.float32, 0.0, upper))
    channel_scale = jnp.exp(jax.random.uniform(key_channel, (1, 1, 1, CHANNELS), jnp.float32, 0.0, upper))
    return base * pixel_scale * channel_scale


def touch_ends(array, stream_key, low, high):
    dims = array.shape
    spot = [jax.random.randint(jax.random.fold_in(stream_key, axis), (), 0, dims[axis]) for axis in range(len(dims))]
    array = array.at[tuple(spot)].set(low)
    longest = dims.index(max(dims))
    spot[longest] = (spot[longest] + 1) % dims[longest]
    return array.at[tuple(spot)].set(high)


def setup_inputs(seed: int = 0) -> dict:
    keys = jax.random.split(jax.random.key(seed), 4)
    facets = draw_facets(jax.random.fold_in(keys[3], 71), 0)
    profiles = jnp.clip(jax.random.uniform(keys[1], (NPROF, FCOLS), jnp.float32, 0.25, 1.0), 0.25, 1.0)
    profile_index = touch_ends(jax.random.randint(keys[2], (FACETS, ROWS), 0, NPROF), jax.random.fold_in(keys[2], 1), 0, NPROF - 1).astype(jnp.int32)
    return dict(facets=facets, profiles=profiles, profile_index=profile_index)


highest = lax.Precision.HIGHEST
epsilon = 1e-06

def facet_step(cube, weight):
    weighted = cube * weight[:, :, None]
    by_channel = weighted.reshape(-1, CHANNELS)
    gram = jnp.dot(by_channel.T, by_channel, precision=highest, preferred_element_type=jnp.float32)
    identity = jnp.eye(CHANNELS, dtype=jnp.float32)
    mean_eig = jnp.trace(gram) / CHANNELS
    moved = gram - mean_eig * identity
    spread = jnp.sqrt(jnp.sum(moved * moved) + epsilon)
    signs = moved / spread
    for iteration in range(ITERS):
        square = jnp.dot(signs, signs, precision=highest, preferred_element_type=jnp.float32)
        cubic = jnp.dot(square, signs, precision=highest, preferred_element_type=jnp.float32)
        signs = 1.5 * signs - 0.5 * cubic
    project = 0.5 * (identity + signs)
    result = jnp.dot(by_channel, project, precision=highest, preferred_element_type=jnp.float32)
    return weight[:, :, None] * result.reshape(cube.shape)

def reference(facets, profiles, profile_index):
    pieces = []
    for facet_id in range(FACETS):
        weight = profiles[profile_index[facet_id]]
        pieces.append(facet_step(facets[facet_id], weight))
    stacked = jnp.stack(pieces, 0)
    zero_rim = jnp.zeros_like(stacked[:1, :, :OV])
    from_left = jnp.concatenate([zero_rim, stacked[:-1, :, FCOLS - OV:]], 0)
    from_right = jnp.concatenate([stacked[1:, :, :OV], zero_rim], 0)
    summed = stacked.at[:, :, :OV].add(from_left)
    summed = summed.at[:, :, FCOLS - OV:].add(from_right)
    return summed
```

```python
import functools

import jax
import jax.numpy as jnp
from jax import lax
from jax.experimental import pallas as pl
from jax.experimental.pallas import tpu as pltpu
from jax.sharding import PartitionSpec as P

OV = 128
ITERS = 4
EPSILON = 1e-06
MESH = pl.DeviceIdType.MESH
BF16 = jnp.bfloat16
F32 = jnp.float32

ROWS = 3
COLS = 1024
BLOCK = 256
HALF = 128
BLOCKS = 4
CHANNELS = BLOCK * BLOCKS
PIXELS = ROWS * BLOCK
PAIRS = [(0, 0), (1, 1), (2, 2), (3, 3), (0, 1), (1, 2), (2, 3), (3, 0), (0, 2), (1, 3)]
TILES = len(PAIRS)


def dot(a, b):
    return lax.dot_general(a, b, (((1,), (0,)), ((), ())), preferred_element_type=F32)


def dot3(a_high, a_low, b_high, b_low):
    return dot(a_high, b_high) + dot(a_high, b_low) + dot(a_low, b_high)


def split(value):
    high = value.astype(BF16)
    low = (value - high.astype(F32)).astype(BF16)
    return high, low


def block(i):
    return slice(i * BLOCK, (i + 1) * BLOCK)


def kernel(
    facets, profiles, index, out,
    cube, weight, pix_hl, pix_t_hl, gram, total, from_core, from_z1, from_z2, from_x,
    signs, square, proj, result, border,
    send_near, recv_near, send_far, recv_far, own_sem,
    send_core, recv_core, send_z, recv_z, send_x, recv_x,
    send_xg, recv_xg, send_zg, recv_zg, send_cg, recv_cg,
    send_border, recv_border, out_sem,
):
    f = lax.axis_index("facet")
    p = lax.axis_index("pix")
    a = lax.axis_index("chan")
    z = p // 2
    k = p % 2
    right = (a + 1) % 4
    left = (a + 3) % 4
    across = (a + 2) % 4
    z_up = (z + 1) % 4
    z_down = (z + 3) % 4
    z_across = (z + 2) % 4

    def at_x(chan):
        return (f, p, chan)

    def at_z(zz):
        return (f, zz * 2 + k, a)

    core_mate = (f, z * 2 + (1 - k), a)
    facet_up = ((f + 1) % 4, p, a)
    facet_down = ((f + 3) % 4, p, a)

    barrier = pltpu.get_barrier_semaphore()
    partners = [
        at_x(right), at_x(left), at_x(across), at_z(z_up), at_z(z_down), core_mate, facet_up, facet_down,
    ]
    for partner in partners:
        pl.semaphore_signal(barrier, inc=1, device_id=partner, device_id_type=MESH)
    pl.semaphore_wait(barrier, len(partners))

    def remote(src, dst, send_sem, recv_sem, device):
        return pltpu.make_async_remote_copy(
            src_ref=src, dst_ref=dst, send_sem=send_sem, recv_sem=recv_sem,
            device_id=device, device_id_type=MESH,
        )

    toward = [right, left]
    behind = [left, right]

    def piece(q, h):
        return pl.ds(pl.multiple_of(q * BLOCK + h * HALF, HALF), HALF)

    def near(way, q, h):
        there = cube.at[a, :, piece(q, h), :]
        return remote(
            facets.at[0, :, piece(q, h), :], there,
            send_near.at[way, q, h], recv_near.at[way, q, h], at_x(toward[way]),
        )

    def far(way, q):
        there = cube.at[behind[way], :, piece(q, way), :]
        return remote(there, there, send_far.at[way, q], recv_far.at[way, q], at_x(toward[way]))

    def wait_near(way, q, h):
        there = cube.at[behind[way], :, piece(q, h), :]
        remote(
            there, there, send_near.at[way, q, h], recv_near.at[way, q, h], at_x(toward[way])
        ).wait_recv()

    def wait_far(way, q):
        there = cube.at[across, :, piece(q, way), :]
        remote(there, there, send_far.at[way, q], recv_far.at[way, q], at_x(toward[way])).wait_recv()

    def quarter(way, step):
        if way == 0:
            place = (4 - right) % 4
            n = step + jnp.where(place <= step, 1, 0)
            return (4 - n) % 4
        place = (left + 1) % 4
        n = step + jnp.where(place <= step, 1, 0)
        return (3 + n) % 4

    def near_round(step):
        for way in (0, 1):
            q = quarter(way, step)
            for h in (way, 1 - way):
                if h == way:
                    @pl.when(q != across)
                    def _():
                        near(way, q, h).start()
                else:
                    near(way, q, h).start()

    def far_round(step):
        for way in (0, 1):
            q = quarter(way, step)

            @pl.when(q != a)
            def _():
                wait_near(way, q, way)

            far(way, q).start()

    for way in (0, 1):
        near(way, toward[way], way).start()
    for way in (0, 1):
        near(way, across, way).start()
    for way in (0, 1):
        near(way, toward[way], 1 - way).start()
    own = pltpu.make_async_copy(facets.at[0], cube.at[a], own_sem)
    own.start()

    for r in range(ROWS):
        row = profiles[0:1, :]
        for n in range(1, profiles.shape[0]):
            row = jnp.where(index[0, r] == n, profiles[n : n + 1, :], row)
        weight[r] = jnp.broadcast_to(row, (128, COLS)).T

    own.wait()

    mine = pl.ds(pl.multiple_of(a * BLOCK, BLOCK), BLOCK)

    def spectra(b):
        columns = pl.ds(pl.multiple_of(b * BLOCK, BLOCK), BLOCK)
        for r in range(ROWS):
            w = weight[r, mine, :]
            x = cube[b, r, mine, :] * jnp.concatenate([w, w], axis=1)
            high, low = split(x)
            pix_hl[0, block(r), columns] = high
            pix_hl[1, block(r), columns] = low
            high, low = split(x.T)
            pix_t_hl[0, columns, block(r)] = high
            pix_t_hl[1, columns, block(r)] = low

    spectra(a)
    for way in (0, 1):
        wait_near(way, toward[way], way)
        far(way, toward[way]).start()
    for way in (0, 1):
        wait_near(way, a, 0)
        wait_near(way, a, 1)
    spectra(left)
    spectra(right)
    for way in (0, 1):
        wait_far(way, a)
    near_round(0)
    spectra(across)

    for t, (i, j) in enumerate(PAIRS):
        gram[t] = dot3(
            pix_t_hl[0, block(i), :], pix_t_hl[1, block(i), :], pix_hl[0, :, block(j)], pix_hl[1, :, block(j)]
        )

    def rows(start, count):
        return pl.ds(pl.multiple_of(start, 8), count)

    half = k * 128
    swap = remote(
        gram.at[:, rows((1 - k) * 128, 128), :], from_core, send_core, recv_core, core_mate
    )
    swap.start()
    swap.wait()

    def part(zz):
        return half + zz * 32

    gram[:, rows(half, 128), :] += from_core[...]

    first = [
        remote(gram.at[:, rows(part(z_across), 16), :], from_z1.at[0], send_z.at[0], recv_z.at[0], at_z(z_up)),
        remote(gram.at[:, rows(part(z_across) + 16, 16), :], from_z1.at[1], send_z.at[1], recv_z.at[1], at_z(z_down)),
    ]
    for copy in first:
        copy.start()
    for copy in first:
        copy.wait()
    gram[:, rows(part(z_up), 16), :] += from_z1[0]
    gram[:, rows(part(z_down) + 16, 16), :] += from_z1[1]
    second = [
        remote(gram.at[:, rows(part(z_up), 32), :], from_z2.at[0], send_z.at[2], recv_z.at[2], at_z(z_up)),
        remote(gram.at[:, rows(part(z_down), 32), :], from_z2.at[1], send_z.at[3], recv_z.at[3], at_z(z_down)),
    ]
    for copy in second:
        copy.start()
    for copy in second:
        copy.wait()
    base = part(z)
    gram[:, rows(base, 32), :] += from_z2[0] + from_z2[1]

    scatter = []
    for d in (1, 2, 3):
        target = (a + d) % 4
        scatter.append(remote(
            gram.at[:, rows(base + target * 8, 8), :], from_x.at[d - 1],
            send_x.at[d - 1], recv_x.at[d - 1], at_x(target),
        ))
    for copy in scatter:
        copy.start()
    for copy in scatter:
        copy.wait()
    own_rows = rows(base + a * 8, 8)
    total[:, own_rows, :] = (gram[:, own_rows, :] + from_x[0]) + (from_x[1] + from_x[2])

    def gather_x(d):
        return remote(
            total.at[:, own_rows, :], total.at[:, own_rows, :],
            send_xg.at[d - 1], recv_xg.at[d - 1], at_x((a + d) % 4),
        )

    for d in (1, 2, 3):
        gather_x(d).start()
    for d in (1, 2, 3):
        there = total.at[:, rows(base + ((a + 4 - d) % 4) * 8, 8), :]
        remote(there, there, send_xg.at[d - 1], recv_xg.at[d - 1], at_x((a + d) % 4)).wait_recv()

    def whole(zz):
        return total.at[:, rows(part(zz), 32), :]

    def low_half(zz):
        return total.at[:, rows(part(zz), 16), :]

    def high_half(zz):
        return total.at[:, rows(part(zz) + 16, 16), :]

    def along(ref, slot, device):
        return remote(ref, ref, send_zg.at[slot], recv_zg.at[slot], device)

    def to_mate(ref, slot):
        return remote(ref, ref, send_cg.at[slot], recv_cg.at[slot], core_mate)

    along(whole(z), 0, at_z(z_up)).start()
    along(whole(z), 1, at_z(z_down)).start()
    to_mate(whole(z), 0).start()
    far_round(0)
    near_round(1)
    near_round(2)
    along(whole(z_down), 0, at_z(z_up)).wait_recv()
    along(low_half(z_down), 2, at_z(z_up)).start()
    to_mate(whole(z_down), 1).start()
    along(whole(z_up), 1, at_z(z_down)).wait_recv()
    along(high_half(z_up), 3, at_z(z_down)).start()
    to_mate(whole(z_up), 2).start()
    along(low_half(z_across), 2, at_z(z_up)).wait_recv()
    along(high_half(z_across), 3, at_z(z_down)).wait_recv()
    to_mate(whole(z_across), 3).start()

    def mate_whole(zz):
        return total.at[:, rows((1 - k) * 128 + zz * 32, 32), :]

    for slot, zz in enumerate((z, z_down, z_up, z_across)):
        to_mate(mate_whole(zz), slot).wait_recv()

    eye = (
        lax.broadcasted_iota(jnp.int32, (BLOCK, BLOCK), 0) == lax.broadcasted_iota(jnp.int32, (BLOCK, BLOCK), 1)
    ).astype(F32)

    def add_up(tile):
        return jnp.sum(jnp.sum(tile, axis=0, keepdims=True), axis=1, keepdims=True)

    diagonal = total[0] * eye
    for t in range(1, BLOCKS):
        diagonal = diagonal + total[t] * eye
    mean_eig = add_up(diagonal) / CHANNELS
    squares = None
    for t in range(TILES):
        if t < BLOCKS:
            moved = total[t] - mean_eig * eye
            term = moved * moved
        else:
            term = 2.0 * (total[t] * total[t])
        squares = term if squares is None else squares + term
    spread = jnp.sqrt(add_up(squares) + EPSILON)

    def put(ref, lead, i, j, tile):
        high, low = split(tile)
        ref[lead + (0, block(i), block(j))] = high
        ref[lead + (1, block(i), block(j))] = low
        if i != j:
            high, low = split(tile.T)
            ref[lead + (0, block(j), block(i))] = high
            ref[lead + (1, block(j), block(i))] = low

    for t, (i, j) in enumerate(PAIRS):
        tile = total[t]
        if i == j:
            tile = tile - mean_eig * eye
        tile = tile / spread
        gram[t] = tile
        put(signs, (0,), i, j, tile)

    def iterate(step, _):
        now = step % 2
        later = 1 - now

        @pl.when(step == 1)
        def _():
            far_round(1)

        @pl.when(step == 2)
        def _():
            far_round(2)

        for i, j in PAIRS:
            put(square, (), i, j, dot3(
                signs[now, 0, block(i), :], signs[now, 1, block(i), :],
                signs[now, 0, :, block(j)], signs[now, 1, :, block(j)],
            ))
        for t, (i, j) in enumerate(PAIRS):
            cubic = dot3(
                signs[now, 0, block(i), :], signs[now, 1, block(i), :],
                square[0, :, block(j)], square[1, :, block(j)],
            )
            tile = 1.5 * gram[t] - 0.5 * cubic
            gram[t] = tile
            put(signs, (later,), i, j, tile)
        return 0

    lax.fori_loop(0, ITERS - 1, iterate, 0)

    last = (ITERS - 1) % 2
    for i in range(BLOCKS):
        high, low = split(dot3(
            signs[last, 0, block(i), :], signs[last, 1, block(i), :],
            signs[last, 0, :, mine], signs[last, 1, :, mine],
        ))
        square[0, block(i), 0:BLOCK] = high
        square[1, block(i), 0:BLOCK] = low
    for i in range(BLOCKS):
        cubic = dot3(
            signs[last, 0, block(i), :], signs[last, 1, block(i), :],
            square[0, :, 0:BLOCK], square[1, :, 0:BLOCK],
        )
        current = signs[last, 0, block(i), mine].astype(F32) + signs[last, 1, block(i), mine].astype(F32)
        high, low = split(1.5 * current - 0.5 * cubic)
        proj[0, block(i), :] = high
        proj[1, block(i), :] = low

    def filtered(q):
        @pl.when(q != a)
        def _():
            for way in (0, 1):
                wait_near(way, q, 1 - way)
                wait_far(way, q)

        for r in range(ROWS):
            x = jnp.concatenate([cube[b, r, block(q), :] for b in range(BLOCKS)], axis=1)
            high, low = split(x)
            product = dot3(high, low, proj[0], proj[1])
            w = weight[r, block(q), :]
            w = 0.5 * (w * w)
            result[r, block(q), :] = (cube[a, r, block(q), :] + product) * jnp.concatenate([w, w], axis=1)

    def to_hbm(q):
        there = (slice(None), block(q), slice(None))
        return pltpu.make_async_copy(result.at[there], out.at[(0,) + there], out_sem.at[q])

    low_rim = result.at[:, 0:OV, :]
    high_rim = result.at[:, COLS - OV : COLS, :]
    down = remote(low_rim, border.at[1], send_border.at[0], recv_border.at[0], facet_down)
    up = remote(high_rim, border.at[0], send_border.at[1], recv_border.at[1], facet_up)

    filtered(0)

    @pl.when(f > 0)
    def _():
        down.start()

    filtered(3)

    @pl.when(f < 3)
    def _():
        up.start()

    for q in (1, 2):
        filtered(q)
        to_hbm(q).start()

    @pl.when(f > 0)
    def _():
        down.wait_send()
        up.wait_recv()
        result[:, 0:OV, :] += border[0]

    to_hbm(0).start()

    @pl.when(f < 3)
    def _():
        up.wait_send()
        down.wait_recv()
        result[:, COLS - OV : COLS, :] += border[1]

    to_hbm(3).start()

    for way in (0, 1):
        for q in range(BLOCKS):
            for h in (0, 1):
                near(way, q, h).wait_send()
            far(way, q).wait_send()
    for d in (1, 2, 3):
        gather_x(d).wait_send()
    along(whole(z), 0, at_z(z_up)).wait_send()
    along(whole(z), 1, at_z(z_down)).wait_send()
    along(low_half(z_down), 2, at_z(z_up)).wait_send()
    along(high_half(z_up), 3, at_z(z_down)).wait_send()
    for slot, zz in enumerate((z, z_down, z_up, z_across)):
        to_mate(whole(zz), slot).wait_send()
    for q in range(BLOCKS):
        to_hbm(q).wait()


def body(facets, profiles, profile_index):
    dma = pltpu.SemaphoreType.DMA
    scratch = [
        pltpu.VMEM((BLOCKS, ROWS, COLS, BLOCK), F32),
        pltpu.VMEM((ROWS, COLS, 128), F32),
        pltpu.VMEM((2, PIXELS, CHANNELS), BF16),
        pltpu.VMEM((2, CHANNELS, PIXELS), BF16),
        pltpu.VMEM((TILES, BLOCK, BLOCK), F32),
        pltpu.VMEM((TILES, BLOCK, BLOCK), F32),
        pltpu.VMEM((TILES, 128, BLOCK), F32),
        pltpu.VMEM((2, TILES, 16, BLOCK), F32),
        pltpu.VMEM((2, TILES, 32, BLOCK), F32),
        pltpu.VMEM((3, TILES, 8, BLOCK), F32),
        pltpu.VMEM((2, 2, CHANNELS, CHANNELS), BF16),
        pltpu.VMEM((2, CHANNELS, CHANNELS), BF16),
        pltpu.VMEM((2, CHANNELS, BLOCK), BF16),
        pltpu.VMEM((ROWS, COLS, BLOCK), F32),
        pltpu.VMEM((2, ROWS, OV, BLOCK), F32),
        dma((2, 4, 2)), dma((2, 4, 2)), dma((2, 4)), dma((2, 4)), dma,
        dma, dma, dma((4,)), dma((4,)), dma((3,)), dma((3,)),
        dma((3,)), dma((3,)), dma((4,)), dma((4,)), dma((4,)), dma((4,)),
        dma((2,)), dma((2,)), dma((4,)),
    ]
    return pl.pallas_call(
        kernel,
        out_shape=jax.ShapeDtypeStruct(facets.shape, F32),
        in_specs=[
            pl.BlockSpec(memory_space=pl.ANY),
            pl.BlockSpec(memory_space=pltpu.VMEM),
            pl.BlockSpec(memory_space=pltpu.SMEM),
        ],
        out_specs=pl.BlockSpec(memory_space=pl.ANY),
        scratch_shapes=scratch,
        compiler_params=pltpu.CompilerParams(
            collective_id=0, has_side_effects=True, vmem_limit_bytes=60 * 2**20
        ),
        cost_estimate=pl.CostEstimate(flops=60 * 10**9, bytes_accessed=6 * 2**20, transcendentals=0),
        name="facet_filter",
    )(facets, profiles, profile_index)


def solution(mesh):
    return jax.shard_map(
        body,
        mesh=mesh,
        in_specs=(P("facet", "pix", None, "chan"), P(), P("facet", "pix")),
        out_specs=P("facet", "pix", None, "chan"),
        check_vma=False,
    )
```

```python
import functools

import jax
import jax.numpy as jnp
from jax import lax
from jax.experimental import pallas as pl
from jax.experimental.pallas import tpu as pltpu
from jax.sharding import PartitionSpec as P

OV = 128
ITERS = 4
EPSILON = 1e-06
MESH = pl.DeviceIdType.MESH
BF16 = jnp.bfloat16
F32 = jnp.float32

ROWS = 3
COLS = 1024
BLOCK = 256
HALF = 128
BLOCKS = 4
CHANNELS = BLOCK * BLOCKS
PIXELS = ROWS * BLOCK
STRIPS = 4
PAIRS = [(0, 0), (1, 1), (2, 2), (3, 3), (0, 1), (1, 2), (2, 3), (3, 0), (0, 2), (1, 3)]
TILES = len(PAIRS)


def dot(a, b):
    return lax.dot_general(a, b, (((1,), (0,)), ((), ())), preferred_element_type=F32)


def dot3(a_high, a_low, b_high, b_low):
    return dot(a_high, b_high) + dot(a_high, b_low) + dot(a_low, b_high)


def split(value):
    high = value.astype(BF16)
    low = (value - high.astype(F32)).astype(BF16)
    return high, low


def block(i):
    return slice(i * BLOCK, (i + 1) * BLOCK)


def kernel(
    facets, profiles, index, out,
    cube, weight, pix_hl, pix_t_hl, gram, total, from_core, from_z1, from_z2, from_x,
    signs, square, latest, proj, result, border, outgoing, incoming,
    send_near, recv_near, send_far, recv_far, own_sem,
    send_core, recv_core, send_z, recv_z, send_x, recv_x,
    send_xg, recv_xg, send_zg, recv_zg, send_cg, recv_cg,
    send_border, recv_border, out_sem, send_tiles, recv_tiles,
):
    f = lax.axis_index("facet")
    p = lax.axis_index("pix")
    a = lax.axis_index("chan")
    z = p // 2
    k = p % 2
    right = (a + 1) % 4
    left = (a + 3) % 4
    across = (a + 2) % 4
    z_up = (z + 1) % 4
    z_down = (z + 3) % 4
    z_across = (z + 2) % 4

    def at_x(chan):
        return (f, p, chan)

    def at_z(zz):
        return (f, zz * 2 + k, a)

    core_mate = (f, z * 2 + (1 - k), a)
    facet_up = ((f + 1) % 4, p, a)
    facet_down = ((f + 3) % 4, p, a)

    barrier = pltpu.get_barrier_semaphore()
    partners = [
        at_x(right), at_x(left), at_x(across), at_z(z_up), at_z(z_down), core_mate, facet_up, facet_down,
    ]
    for partner in partners:
        pl.semaphore_signal(barrier, inc=1, device_id=partner, device_id_type=MESH)
    pl.semaphore_wait(barrier, len(partners))

    def remote(src, dst, send_sem, recv_sem, device):
        return pltpu.make_async_remote_copy(
            src_ref=src, dst_ref=dst, send_sem=send_sem, recv_sem=recv_sem,
            device_id=device, device_id_type=MESH,
        )

    toward = [right, left]
    behind = [left, right]

    def piece(q, h):
        return pl.ds(pl.multiple_of(q * BLOCK + h * HALF, HALF), HALF)

    def near(way, q, h):
        there = cube.at[a, :, piece(q, h), :]
        return remote(
            facets.at[0, :, piece(q, h), :], there,
            send_near.at[way, q, h], recv_near.at[way, q, h], at_x(toward[way]),
        )

    def far(way, q):
        there = cube.at[behind[way], :, piece(q, way), :]
        return remote(there, there, send_far.at[way, q], recv_far.at[way, q], at_x(toward[way]))

    def wait_near(way, q, h):
        there = cube.at[behind[way], :, piece(q, h), :]
        remote(
            there, there, send_near.at[way, q, h], recv_near.at[way, q, h], at_x(toward[way])
        ).wait_recv()

    def wait_far(way, q):
        there = cube.at[across, :, piece(q, way), :]
        remote(there, there, send_far.at[way, q], recv_far.at[way, q], at_x(toward[way])).wait_recv()

    def place(way, q):
        return (4 - q) % 4 if way == 0 else (q + 1) % 4

    def quarter(way, step):
        n = step + jnp.where(place(way, toward[way]) <= step, 1, 0)
        return (4 - n) % 4 if way == 0 else (3 + n) % 4

    def near_item(item, strips=(0, STRIPS)):
        for way in (0, 1):
            n = place(way, across)
            skipped = 2 * (n - jnp.where(place(way, toward[way]) <= n, 1, 0))
            m = item + jnp.where(skipped <= item, 1, 0)
            h = m % 2 if way == 0 else 1 - m % 2
            q = quarter(way, m // 2)
            width = HALF // STRIPS
            strip = pl.ds(
                pl.multiple_of(q * BLOCK + h * HALF + strips[0] * width, width), (strips[1] - strips[0]) * width
            )
            remote(
                facets.at[0, :, strip, :], cube.at[a, :, strip, :],
                send_near.at[way, q, h], recv_near.at[way, q, h], at_x(toward[way]),
            ).start()

    def far_round(step):
        for way in (0, 1):
            q = quarter(way, step)

            @pl.when(q != a)
            def _():
                wait_near(way, q, way)

            far(way, q).start()

    for h in (0, 1):
        for way in (0, 1):
            near(way, toward[way], h).start()
    for way in (0, 1):
        near(way, across, way).start()
    own = pltpu.make_async_copy(facets.at[0], cube.at[a], own_sem)
    own.start()

    for r in range(ROWS):
        row = profiles[0:1, :]
        for n in range(1, profiles.shape[0]):
            row = jnp.where(index[0, r] == n, profiles[n : n + 1, :], row)
        weight[r] = jnp.broadcast_to(row, (128, COLS)).T

    own.wait()

    mine = pl.ds(pl.multiple_of(a * BLOCK, BLOCK), BLOCK)

    def spectra(b, distance):
        for r in range(ROWS):
            w = weight[r, mine, :]
            x = cube[b, r, mine, :] * jnp.concatenate([w, w], axis=1)
            high, low = split(x)
            pix_hl[0, block(r), block(distance)] = high
            pix_hl[1, block(r), block(distance)] = low
            high, low = split(x.T)
            pix_t_hl[0, block(distance), block(r)] = high
            pix_t_hl[1, block(distance), block(r)] = low

    def gram_tile(slot, i, j):
        gram[slot] = dot3(pix_t_hl[0, i, :], pix_t_hl[1, i, :], pix_hl[0, :, j], pix_hl[1, :, j])

    def distant(d):
        return pl.ds(pl.multiple_of(d * BLOCK, BLOCK), BLOCK)

    SPANS = [pl.ds(0, 6), pl.ds(6, 4)]

    def rows(start, count):
        return pl.ds(pl.multiple_of(start, 8), count)

    half = k * 128

    def part(zz):
        return half + zz * 32

    def swap(e):
        return remote(
            gram.at[SPANS[e], rows((1 - k) * 128, 128), :], from_core.at[SPANS[e]],
            send_core.at[e], recv_core.at[e], core_mate,
        )

    def sixteen(e, zz, h):
        return gram.at[SPANS[e], rows(part(zz) + 16 * h, 16), :]

    z_to = [z_up, z_down]

    def first(e, way):
        return remote(
            sixteen(e, z_across, way), from_z1.at[way, SPANS[e]],
            send_z.at[e, way, 0], recv_z.at[e, way, 0], at_z(z_to[way]),
        )

    def second(e, way, h):
        return remote(
            sixteen(e, z_to[way], h), from_z2.at[way, h, SPANS[e]],
            send_z.at[e, way, 1 + h], recv_z.at[e, way, 1 + h], at_z(z_to[way]),
        )

    def cores_summed(e):
        swap(e).start()
        swap(e).wait()
        gram[SPANS[e], rows(half, 128), :] += from_core[SPANS[e]]
        for way in (0, 1):
            first(e, way).start()
        for way in (0, 1):
            second(e, way, 1 - way).start()

    def z_summed(e):
        for way in (0, 1):
            first(e, way).wait_recv()
            gram[SPANS[e], rows(part(z_to[way]) + 16 * way, 16), :] += from_z1[way, SPANS[e]]
            second(e, way, way).start()
        for h in (0, 1):
            second(e, 0, h).wait_recv()
            second(e, 1, h).wait_recv()
            gram[SPANS[e], rows(part(z) + 16 * h, 16), :] += from_z2[0, h, SPANS[e]] + from_z2[1, h, SPANS[e]]

    spectra(a, 0)
    gram_tile(1, block(0), block(0))
    for way in (0, 1):
        wait_near(way, a, 0)
        wait_near(way, a, 1)
    spectra(left, 3)
    spectra(right, 1)
    gram_tile(0, block(3), block(3))
    gram_tile(2, block(1), block(1))
    gram_tile(3, block(3), block(0))
    gram_tile(4, block(0), block(1))
    side = jnp.where((a == 0) | (a == 3), 1, 3)
    gram_tile(5, distant(side), distant(4 - side))
    cores_summed(0)
    for way in (0, 1):
        wait_near(way, toward[way], way)
        far(way, toward[way]).start()
    near_item(0)
    z_summed(0)
    for way in (0, 1):
        wait_far(way, a)
    spectra(across, 2)
    gram_tile(6, block(2), block(2))
    gram_tile(7, block(1), block(2))
    gram_tile(8, block(2), block(3))
    side = jnp.where(a < 2, 0, 2)
    gram_tile(9, distant(side), distant(2 - side))
    cores_summed(1)
    near_item(1, (0, 2))
    z_summed(1)
    base = part(z)

    scatter = []
    for d in (1, 2, 3):
        target = (a + d) % 4
        scatter.append(remote(
            gram.at[:, rows(base + target * 8, 8), :], from_x.at[d - 1],
            send_x.at[d - 1], recv_x.at[d - 1], at_x(target),
        ))
    for copy in scatter:
        copy.start()
    near_item(1, (2, 3))
    for copy in scatter:
        copy.wait()
    own_rows = rows(base + a * 8, 8)

    def pick(n, values):
        result = values[0]
        for m in range(1, len(values)):
            result = jnp.where(n == m, values[m], result)
        return result

    def slot(chan, t):
        if t < 4:
            return pick((t + 4 - chan) % 4, [1, 2, 6, 0])
        if t < 8:
            return pick((t - chan) % 4, [4, 7, 8, 3])
        return pick((t + chan) % 2, [9, 5])

    for t in range(TILES):
        total[t, own_rows, :] = (
            gram[slot(a, t), own_rows, :] + from_x[0, slot(left, t)]
        ) + (from_x[1, slot(across, t)] + from_x[2, slot(right, t)])

    def gather_x(d):
        return remote(
            total.at[:, own_rows, :], total.at[:, own_rows, :],
            send_xg.at[d - 1], recv_xg.at[d - 1], at_x((a + d) % 4),
        )

    for d in (1, 2, 3):
        gather_x(d).start()
    for d in (1, 2, 3):
        there = total.at[:, rows(base + ((a + 4 - d) % 4) * 8, 8), :]
        remote(there, there, send_xg.at[d - 1], recv_xg.at[d - 1], at_x((a + d) % 4)).wait_recv()

    def whole(zz):
        return total.at[:, rows(part(zz), 32), :]

    def low_half(zz):
        return total.at[:, rows(part(zz), 16), :]

    def high_half(zz):
        return total.at[:, rows(part(zz) + 16, 16), :]

    def along(ref, slot, device):
        return remote(ref, ref, send_zg.at[slot], recv_zg.at[slot], device)

    def to_mate(ref, slot):
        return remote(ref, ref, send_cg.at[slot], recv_cg.at[slot], core_mate)

    along(low_half(z), 0, at_z(z_up)).start()
    along(high_half(z), 3, at_z(z_down)).start()
    along(high_half(z), 1, at_z(z_up)).start()
    along(low_half(z), 4, at_z(z_down)).start()
    to_mate(whole(z), 0).start()
    near_item(1, (3, 4))
    far_round(0)
    near_item(2)
    near_item(3)
    near_item(4)
    along(low_half(z_down), 0, at_z(z_up)).wait_recv()
    along(low_half(z_down), 2, at_z(z_up)).start()
    along(high_half(z_up), 3, at_z(z_down)).wait_recv()
    along(high_half(z_up), 5, at_z(z_down)).start()
    along(high_half(z_down), 1, at_z(z_up)).wait_recv()
    to_mate(whole(z_down), 1).start()
    along(low_half(z_up), 4, at_z(z_down)).wait_recv()
    to_mate(whole(z_up), 2).start()
    along(low_half(z_across), 2, at_z(z_up)).wait_recv()
    along(high_half(z_across), 5, at_z(z_down)).wait_recv()
    to_mate(whole(z_across), 3).start()

    def mate_whole(zz):
        return total.at[:, rows((1 - k) * 128 + zz * 32, 32), :]

    for slot, zz in enumerate((z, z_down, z_up, z_across)):
        to_mate(mate_whole(zz), slot).wait_recv()

    eye = (
        lax.broadcasted_iota(jnp.int32, (BLOCK, BLOCK), 0) == lax.broadcasted_iota(jnp.int32, (BLOCK, BLOCK), 1)
    ).astype(F32)

    def add_up(tile):
        return jnp.sum(jnp.sum(tile, axis=0, keepdims=True), axis=1, keepdims=True)

    diagonal = total[0] * eye
    for t in range(1, BLOCKS):
        diagonal = diagonal + total[t] * eye
    mean_eig = add_up(diagonal) / CHANNELS
    squares = None
    for t in range(TILES):
        if t < BLOCKS:
            moved = total[t] - mean_eig * eye
            term = moved * moved
        else:
            term = 2.0 * (total[t] * total[t])
        squares = term if squares is None else squares + term
    spread = jnp.sqrt(add_up(squares) + EPSILON)

    def put(ref, lead, i, j, tile, mirror):
        high, low = split(tile)
        ref[lead + (0, i, j)] = high
        ref[lead + (1, i, j)] = low
        if mirror:
            high, low = split(tile.T)
            ref[lead + (0, j, i)] = high
            ref[lead + (1, j, i)] = low

    def local(b):
        return pl.ds(pl.multiple_of(((b + 2 * k) % 4) * BLOCK, BLOCK), BLOCK)

    for t, (i, j) in enumerate(PAIRS):
        tile = total[t]
        if i == j:
            tile = tile - mean_eig * eye
        put(signs, (0,), local(i), local(j), tile / spread, i != j)

    own_tiles = [(0, 0), (0, 1), (1, 1)]
    cross_tiles = [(0, 2), (0, 3), (1, 2), (1, 3)]

    def trade(step):
        return remote(outgoing.at[step], incoming.at[step], send_tiles.at[step], recv_tiles.at[step], core_mate)

    def absorb(step, buffer):
        trade(step).wait_recv()
        for n, (i, j) in enumerate(own_tiles):
            put(signs, (buffer,), block(i + 2), block(j + 2), incoming[step, n], i != j)

    for step in range(ITERS - 1):
        now = step % 2
        later = 1 - now

        def squared(i, j):
            return dot3(
                signs[now, 0, block(i), :], signs[now, 1, block(i), :],
                signs[now, 0, :, block(j)], signs[now, 1, :, block(j)],
            )

        def renewed(i, j):
            cubic = dot3(
                square[0, block(i), :], square[1, block(i), :],
                signs[now, 0, :, block(j)], signs[now, 1, :, block(j)],
            )
            current = signs[now, 0, block(i), block(j)].astype(F32) + signs[now, 1, block(i), block(j)].astype(F32)
            return 1.5 * current - 0.5 * cubic

        for i, j in own_tiles:
            put(square, (), block(i), block(j), squared(i, j), i != j)

        if step > 0:
            absorb(step - 1, now)
        if step == 2:
            far_round(1)

        for i, j in cross_tiles:
            put(square, (), block(i), block(j), squared(i, j), False)
        for n, (i, j) in enumerate(own_tiles):
            tile = renewed(i, j)
            outgoing[step, n] = tile
            put(signs, (later,), block(i), block(j), tile, i != j)
        trade(step).start()
        for i, j in cross_tiles:
            put(signs, (later,), block(i), block(j), renewed(i, j), True)

    last = (ITERS - 1) % 2
    absorb(ITERS - 2, last)
    far_round(2)
    here = local(a)
    for i in range(BLOCKS):
        high, low = split(dot3(
            signs[last, 0, block(i), :], signs[last, 1, block(i), :],
            signs[last, 0, :, here], signs[last, 1, :, here],
        ))
        latest[0, block(i), :] = high
        latest[1, block(i), :] = low
    for i in range(BLOCKS):
        cubic = dot3(
            signs[last, 0, block(i), :], signs[last, 1, block(i), :], latest[0], latest[1],
        )
        current = signs[last, 0, block(i), here].astype(F32) + signs[last, 1, block(i), here].astype(F32)
        high, low = split(1.5 * current - 0.5 * cubic)
        proj[0, block(i), :] = high
        proj[1, block(i), :] = low

    def filtered(q):
        @pl.when(q != a)
        def _():
            for way in (0, 1):
                wait_near(way, q, 1 - way)
                wait_far(way, q)

        for r in range(ROWS):
            x = jnp.concatenate([cube[(b + 2 * k) % 4, r, block(q), :] for b in range(BLOCKS)], axis=1)
            high, low = split(x)
            product = dot3(high, low, proj[0], proj[1])
            w = weight[r, block(q), :]
            w = 0.5 * (w * w)
            result[r, block(q), :] = (cube[a, r, block(q), :] + product) * jnp.concatenate([w, w], axis=1)

    def to_hbm(q):
        there = (slice(None), block(q), slice(None))
        return pltpu.make_async_copy(result.at[there], out.at[(0,) + there], out_sem.at[q])

    low_rim = result.at[:, 0:OV, :]
    high_rim = result.at[:, COLS - OV : COLS, :]
    down = remote(low_rim, border.at[1], send_border.at[0], recv_border.at[0], facet_down)
    up = remote(high_rim, border.at[0], send_border.at[1], recv_border.at[1], facet_up)

    filtered(0)

    @pl.when(f > 0)
    def _():
        down.start()

    filtered(3)

    @pl.when(f < 3)
    def _():
        up.start()

    for q in (1, 2):
        filtered(q)
        to_hbm(q).start()

    @pl.when(f > 0)
    def _():
        down.wait_send()
        up.wait_recv()
        result[:, 0:OV, :] += border[0]

    to_hbm(0).start()

    @pl.when(f < 3)
    def _():
        up.wait_send()
        down.wait_recv()
        result[:, COLS - OV : COLS, :] += border[1]

    to_hbm(3).start()

    for way in (0, 1):
        for q in range(BLOCKS):
            for h in (0, 1):
                near(way, q, h).wait_send()
            far(way, q).wait_send()
    for d in (1, 2, 3):
        gather_x(d).wait_send()
    for way in (0, 1):
        for e in (0, 1):
            first(e, way).wait_send()
            for h in (0, 1):
                second(e, way, h).wait_send()
    along(low_half(z), 0, at_z(z_up)).wait_send()
    along(high_half(z), 1, at_z(z_up)).wait_send()
    along(low_half(z_down), 2, at_z(z_up)).wait_send()
    along(high_half(z), 3, at_z(z_down)).wait_send()
    along(low_half(z), 4, at_z(z_down)).wait_send()
    along(high_half(z_up), 5, at_z(z_down)).wait_send()
    for step in range(ITERS - 1):
        trade(step).wait_send()
    for slot, zz in enumerate((z, z_down, z_up, z_across)):
        to_mate(whole(zz), slot).wait_send()
    for q in range(BLOCKS):
        to_hbm(q).wait()


def body(facets, profiles, profile_index):
    dma = pltpu.SemaphoreType.DMA
    scratch = [
        pltpu.VMEM((BLOCKS, ROWS, COLS, BLOCK), F32),
        pltpu.VMEM((ROWS, COLS, 128), F32),
        pltpu.VMEM((2, PIXELS, CHANNELS), BF16),
        pltpu.VMEM((2, CHANNELS, PIXELS), BF16),
        pltpu.VMEM((TILES, BLOCK, BLOCK), F32),
        pltpu.VMEM((TILES, BLOCK, BLOCK), F32),
        pltpu.VMEM((TILES, 128, BLOCK), F32),
        pltpu.VMEM((2, TILES, 16, BLOCK), F32),
        pltpu.VMEM((2, 2, TILES, 16, BLOCK), F32),
        pltpu.VMEM((3, TILES, 8, BLOCK), F32),
        pltpu.VMEM((2, 2, CHANNELS, CHANNELS), BF16),
        pltpu.VMEM((2, 2 * BLOCK, CHANNELS), BF16),
        pltpu.VMEM((2, CHANNELS, BLOCK), BF16),
        pltpu.VMEM((2, CHANNELS, BLOCK), BF16),
        pltpu.VMEM((ROWS, COLS, BLOCK), F32),
        pltpu.VMEM((2, ROWS, OV, BLOCK), F32),
        pltpu.VMEM((ITERS - 1, 3, BLOCK, BLOCK), F32),
        pltpu.VMEM((ITERS - 1, 3, BLOCK, BLOCK), F32),
        dma((2, 4, 2)), dma((2, 4, 2)), dma((2, 4)), dma((2, 4)), dma,
        dma((2,)), dma((2,)), dma((2, 2, 3)), dma((2, 2, 3)), dma((3,)), dma((3,)),
        dma((3,)), dma((3,)), dma((6,)), dma((6,)), dma((4,)), dma((4,)),
        dma((2,)), dma((2,)), dma((4,)), dma((ITERS - 1,)), dma((ITERS - 1,)),
    ]
    return pl.pallas_call(
        kernel,
        out_shape=jax.ShapeDtypeStruct(facets.shape, F32),
        in_specs=[
            pl.BlockSpec(memory_space=pl.ANY),
            pl.BlockSpec(memory_space=pltpu.VMEM),
            pl.BlockSpec(memory_space=pltpu.SMEM),
        ],
        out_specs=pl.BlockSpec(memory_space=pl.ANY),
        scratch_shapes=scratch,
        compiler_params=pltpu.CompilerParams(
            collective_id=0, has_side_effects=True, vmem_limit_bytes=60 * 2**20
        ),
        cost_estimate=pl.CostEstimate(flops=60 * 10**9, bytes_accessed=6 * 2**20, transcendentals=0),
        name="facet_filter",
    )(facets, profiles, profile_index)


def solution(mesh):
    return jax.shard_map(
        body,
        mesh=mesh,
        in_specs=(P("facet", "pix", None, "chan"), P(), P("facet", "pix")),
        out_specs=P("facet", "pix", None, "chan"),
        check_vma=False,
    )
```

```python
import functools

import jax
import jax.numpy as jnp
from jax import lax
from jax.experimental import pallas as pl
from jax.experimental.pallas import tpu as pltpu
from jax.sharding import PartitionSpec as P

OV = 128
ITERS = 4
EPSILON = 1e-06
MESH = pl.DeviceIdType.MESH
BF16 = jnp.bfloat16
F32 = jnp.float32

ROWS = 3
COLS = 1024
BLOCK = 256
HALF = 128
BLOCKS = 4
CHANNELS = BLOCK * BLOCKS
PIXELS = ROWS * BLOCK
STRIPS = 4
PAIRS = [(0, 0), (1, 1), (2, 2), (3, 3), (0, 1), (1, 2), (2, 3), (3, 0), (0, 2), (1, 3)]
TILES = len(PAIRS)


def dot(a, b):
    return lax.dot_general(a, b, (((1,), (0,)), ((), ())), preferred_element_type=F32)


def dot3(a_high, a_low, b_high, b_low):
    return dot(a_high, b_high) + dot(a_high, b_low) + dot(a_low, b_high)


def split(value):
    high = value.astype(BF16)
    low = (value - high.astype(F32)).astype(BF16)
    return high, low


def block(i):
    return slice(i * BLOCK, (i + 1) * BLOCK)


def kernel(
    facets, profiles, index, out,
    cube, weight, pix_hl, pix_t_hl, gram, total, from_core, from_z1, from_z2, from_x,
    signs, square, latest, proj, result, border, outgoing, incoming,
    send_near, recv_near, send_far, recv_far, own_sem,
    send_core, recv_core, send_z, recv_z, send_x, recv_x,
    send_xg, recv_xg, send_zg, recv_zg, send_cg, recv_cg,
    send_border, recv_border, out_sem, send_tiles, recv_tiles,
):
    f = lax.axis_index("facet")
    p = lax.axis_index("pix")
    a = lax.axis_index("chan")
    z = p // 2
    k = p % 2
    right = (a + 1) % 4
    left = (a + 3) % 4
    across = (a + 2) % 4
    z_up = (z + 1) % 4
    z_down = (z + 3) % 4
    z_across = (z + 2) % 4

    def at_x(chan):
        return (f, p, chan)

    def at_z(zz):
        return (f, zz * 2 + k, a)

    core_mate = (f, z * 2 + (1 - k), a)
    facet_up = ((f + 1) % 4, p, a)
    facet_down = ((f + 3) % 4, p, a)

    barrier = pltpu.get_barrier_semaphore()
    partners = [
        at_x(right), at_x(left), at_x(across), at_z(z_up), at_z(z_down), core_mate, facet_up, facet_down,
    ]
    for partner in partners:
        pl.semaphore_signal(barrier, inc=1, device_id=partner, device_id_type=MESH)
    pl.semaphore_wait(barrier, len(partners))

    def remote(src, dst, send_sem, recv_sem, device):
        return pltpu.make_async_remote_copy(
            src_ref=src, dst_ref=dst, send_sem=send_sem, recv_sem=recv_sem,
            device_id=device, device_id_type=MESH,
        )

    toward = [right, left]
    behind = [left, right]

    def piece(q, h):
        return pl.ds(pl.multiple_of(q * BLOCK + h * HALF, HALF), HALF)

    def near(way, q, h):
        there = cube.at[a, :, piece(q, h), :]
        return remote(
            facets.at[0, :, piece(q, h), :], there,
            send_near.at[way, q, h], recv_near.at[way, q, h], at_x(toward[way]),
        )

    def far(way, q):
        there = cube.at[behind[way], :, piece(q, way), :]
        return remote(there, there, send_far.at[way, q], recv_far.at[way, q], at_x(toward[way]))

    def wait_near(way, q, h):
        there = cube.at[behind[way], :, piece(q, h), :]
        remote(
            there, there, send_near.at[way, q, h], recv_near.at[way, q, h], at_x(toward[way])
        ).wait_recv()

    def wait_far(way, q):
        there = cube.at[across, :, piece(q, way), :]
        remote(there, there, send_far.at[way, q], recv_far.at[way, q], at_x(toward[way])).wait_recv()

    def place(way, q):
        return (4 - q) % 4 if way == 0 else (q + 1) % 4

    def quarter(way, step):
        n = step + jnp.where(place(way, toward[way]) <= step, 1, 0)
        return (4 - n) % 4 if way == 0 else (3 + n) % 4

    def near_item(item, strips=(0, STRIPS)):
        for way in (0, 1):
            n = place(way, across)
            skipped = 2 * (n - jnp.where(place(way, toward[way]) <= n, 1, 0))
            m = item + jnp.where(skipped <= item, 1, 0)
            h = m % 2 if way == 0 else 1 - m % 2
            q = quarter(way, m // 2)
            width = HALF // STRIPS
            strip = pl.ds(
                pl.multiple_of(q * BLOCK + h * HALF + strips[0] * width, width), (strips[1] - strips[0]) * width
            )
            remote(
                facets.at[0, :, strip, :], cube.at[a, :, strip, :],
                send_near.at[way, q, h], recv_near.at[way, q, h], at_x(toward[way]),
            ).start()

    def far_round(step):
        for way in (0, 1):
            q = quarter(way, step)

            @pl.when(q != a)
            def _():
                wait_near(way, q, way)

            far(way, q).start()

    for h in (0, 1):
        for way in (0, 1):
            near(way, toward[way], h).start()
    for way in (0, 1):
        near(way, across, way).start()
    own = pltpu.make_async_copy(facets.at[0], cube.at[a], own_sem)
    own.start()

    for r in range(ROWS):
        row = profiles[0:1, :]
        for n in range(1, profiles.shape[0]):
            row = jnp.where(index[0, r] == n, profiles[n : n + 1, :], row)
        weight[r] = jnp.broadcast_to(row, (128, COLS)).T

    own.wait()

    mine = pl.ds(pl.multiple_of(a * BLOCK, BLOCK), BLOCK)

    def spectra(b, distance):
        for r in range(ROWS):
            w = weight[r, mine, :]
            x = cube[b, r, mine, :] * jnp.concatenate([w, w], axis=1)
            high, low = split(x)
            pix_hl[0, block(r), block(distance)] = high
            pix_hl[1, block(r), block(distance)] = low
            high, low = split(x.T)
            pix_t_hl[0, block(distance), block(r)] = high
            pix_t_hl[1, block(distance), block(r)] = low

    def gram_tile(slot, i, j):
        gram[slot] = dot3(pix_t_hl[0, i, :], pix_t_hl[1, i, :], pix_hl[0, :, j], pix_hl[1, :, j])

    def distant(d):
        return pl.ds(pl.multiple_of(d * BLOCK, BLOCK), BLOCK)

    SPANS = [pl.ds(0, 6), pl.ds(6, 4)]

    def rows(start, count):
        return pl.ds(pl.multiple_of(start, 8), count)

    half = k * 128

    def part(zz):
        return half + zz * 32

    def swap(e):
        return remote(
            gram.at[SPANS[e], rows((1 - k) * 128, 128), :], from_core.at[SPANS[e]],
            send_core.at[e], recv_core.at[e], core_mate,
        )

    def sixteen(e, zz, h):
        return gram.at[SPANS[e], rows(part(zz) + 16 * h, 16), :]

    z_to = [z_up, z_down]

    def first(e, way):
        return remote(
            sixteen(e, z_across, way), from_z1.at[way, SPANS[e]],
            send_z.at[e, way, 0], recv_z.at[e, way, 0], at_z(z_to[way]),
        )

    def second(e, way, h):
        return remote(
            sixteen(e, z_to[way], h), from_z2.at[way, h, SPANS[e]],
            send_z.at[e, way, 1 + h], recv_z.at[e, way, 1 + h], at_z(z_to[way]),
        )

    def cores_summed(e):
        swap(e).start()
        swap(e).wait()
        gram[SPANS[e], rows(half, 128), :] += from_core[SPANS[e]]
        for way in (0, 1):
            first(e, way).start()
        for way in (0, 1):
            second(e, way, 1 - way).start()

    def z_summed(e):
        for way in (0, 1):
            first(e, way).wait_recv()
            gram[SPANS[e], rows(part(z_to[way]) + 16 * way, 16), :] += from_z1[way, SPANS[e]]
            second(e, way, way).start()
        for h in (0, 1):
            second(e, 0, h).wait_recv()
            second(e, 1, h).wait_recv()
            gram[SPANS[e], rows(part(z) + 16 * h, 16), :] += from_z2[0, h, SPANS[e]] + from_z2[1, h, SPANS[e]]

    spectra(a, 0)
    gram_tile(1, block(0), block(0))
    for way in (0, 1):
        wait_near(way, a, 0)
        wait_near(way, a, 1)
    spectra(left, 3)
    spectra(right, 1)
    gram_tile(0, block(3), block(3))
    gram_tile(2, block(1), block(1))
    gram_tile(3, block(3), block(0))
    gram_tile(4, block(0), block(1))
    side = jnp.where((a == 0) | (a == 3), 1, 3)
    gram_tile(5, distant(side), distant(4 - side))
    cores_summed(0)
    for way in (0, 1):
        wait_near(way, toward[way], way)
        far(way, toward[way]).start()
    near_item(0)
    z_summed(0)
    for way in (0, 1):
        wait_far(way, a)
    spectra(across, 2)
    gram_tile(6, block(2), block(2))
    gram_tile(7, block(1), block(2))
    gram_tile(8, block(2), block(3))
    side = jnp.where(a < 2, 0, 2)
    gram_tile(9, distant(side), distant(2 - side))
    cores_summed(1)
    near_item(1, (0, 2))
    z_summed(1)
    base = part(z)

    scatter = []
    for d in (1, 2, 3):
        target = (a + d) % 4
        scatter.append(remote(
            gram.at[:, rows(base + target * 8, 8), :], from_x.at[d - 1],
            send_x.at[d - 1], recv_x.at[d - 1], at_x(target),
        ))
    for copy in scatter:
        copy.start()
    near_item(1, (2, 3))
    for copy in scatter:
        copy.wait()
    own_rows = rows(base + a * 8, 8)

    def pick(n, values):
        result = values[0]
        for m in range(1, len(values)):
            result = jnp.where(n == m, values[m], result)
        return result

    def slot(chan, t):
        if t < 4:
            return pick((t + 4 - chan) % 4, [1, 2, 6, 0])
        if t < 8:
            return pick((t - chan) % 4, [4, 7, 8, 3])
        return pick((t + chan) % 2, [9, 5])

    for t in range(TILES):
        total[t, own_rows, :] = (
            gram[slot(a, t), own_rows, :] + from_x[0, slot(left, t)]
        ) + (from_x[1, slot(across, t)] + from_x[2, slot(right, t)])

    def gather_x(d):
        return remote(
            total.at[:, own_rows, :], total.at[:, own_rows, :],
            send_xg.at[d - 1], recv_xg.at[d - 1], at_x((a + d) % 4),
        )

    for d in (1, 2, 3):
        gather_x(d).start()
    near_item(1, (3, 4))
    far_round(0)
    near_item(2)
    near_item(3)
    for d in (1, 2, 3):
        there = total.at[:, rows(base + ((a + 4 - d) % 4) * 8, 8), :]
        remote(there, there, send_xg.at[d - 1], recv_xg.at[d - 1], at_x((a + d) % 4)).wait_recv()

    def whole(zz):
        return total.at[:, rows(part(zz), 32), :]

    def low_half(zz):
        return total.at[:, rows(part(zz), 16), :]

    def high_half(zz):
        return total.at[:, rows(part(zz) + 16, 16), :]

    def along(ref, slot, device):
        return remote(ref, ref, send_zg.at[slot], recv_zg.at[slot], device)

    def to_mate(ref, slot):
        return remote(ref, ref, send_cg.at[slot], recv_cg.at[slot], core_mate)

    along(low_half(z), 0, at_z(z_up)).start()
    along(high_half(z), 3, at_z(z_down)).start()
    along(high_half(z), 1, at_z(z_up)).start()
    along(low_half(z), 4, at_z(z_down)).start()
    to_mate(whole(z), 0).start()
    along(low_half(z_down), 0, at_z(z_up)).wait_recv()
    along(low_half(z_down), 2, at_z(z_up)).start()
    along(high_half(z_up), 3, at_z(z_down)).wait_recv()
    along(high_half(z_up), 5, at_z(z_down)).start()
    along(high_half(z_down), 1, at_z(z_up)).wait_recv()
    to_mate(whole(z_down), 1).start()
    along(low_half(z_up), 4, at_z(z_down)).wait_recv()
    to_mate(whole(z_up), 2).start()
    along(low_half(z_across), 2, at_z(z_up)).wait_recv()
    along(high_half(z_across), 5, at_z(z_down)).wait_recv()
    to_mate(whole(z_across), 3).start()

    def mate_whole(zz):
        return total.at[:, rows((1 - k) * 128 + zz * 32, 32), :]

    for slot, zz in enumerate((z, z_down, z_up, z_across)):
        to_mate(mate_whole(zz), slot).wait_recv()

    eye = (
        lax.broadcasted_iota(jnp.int32, (BLOCK, BLOCK), 0) == lax.broadcasted_iota(jnp.int32, (BLOCK, BLOCK), 1)
    ).astype(F32)

    def add_up(tile):
        return jnp.sum(jnp.sum(tile, axis=0, keepdims=True), axis=1, keepdims=True)

    diagonal = total[0] * eye
    for t in range(1, BLOCKS):
        diagonal = diagonal + total[t] * eye
    mean_eig = add_up(diagonal) / CHANNELS
    squares = None
    for t in range(TILES):
        if t < BLOCKS:
            moved = total[t] - mean_eig * eye
            term = moved * moved
        else:
            term = 2.0 * (total[t] * total[t])
        squares = term if squares is None else squares + term
    spread = jnp.sqrt(add_up(squares) + EPSILON)

    def put(ref, lead, i, j, tile, mirror):
        high, low = split(tile)
        ref[lead + (0, i, j)] = high
        ref[lead + (1, i, j)] = low
        if mirror:
            high, low = split(tile.T)
            ref[lead + (0, j, i)] = high
            ref[lead + (1, j, i)] = low

    def local(b):
        return pl.ds(pl.multiple_of(((b + 2 * k) % 4) * BLOCK, BLOCK), BLOCK)

    for t, (i, j) in enumerate(PAIRS):
        tile = total[t]
        if i == j:
            tile = tile - mean_eig * eye
        put(signs, (0,), local(i), local(j), tile / spread, i != j)

    own_tiles = [(0, 0), (0, 1), (1, 1)]
    cross_tiles = [(0, 2), (0, 3), (1, 2), (1, 3)]

    def trade(step):
        return remote(outgoing.at[step], incoming.at[step], send_tiles.at[step], recv_tiles.at[step], core_mate)

    def absorb(step, buffer):
        trade(step).wait_recv()
        for n, (i, j) in enumerate(own_tiles):
            put(signs, (buffer,), block(i + 2), block(j + 2), incoming[step, n], i != j)

    for step in range(ITERS - 1):
        now = step % 2
        later = 1 - now

        def squared(i, j):
            return dot3(
                signs[now, 0, block(i), :], signs[now, 1, block(i), :],
                signs[now, 0, :, block(j)], signs[now, 1, :, block(j)],
            )

        def renewed(i, j):
            cubic = dot3(
                square[0, block(i), :], square[1, block(i), :],
                signs[now, 0, :, block(j)], signs[now, 1, :, block(j)],
            )
            current = signs[now, 0, block(i), block(j)].astype(F32) + signs[now, 1, block(i), block(j)].astype(F32)
            return 1.5 * current - 0.5 * cubic

        for i, j in own_tiles:
            put(square, (), block(i), block(j), squared(i, j), i != j)

        if step > 0:
            absorb(step - 1, now)
        if step == 1:
            far_round(1)
            near_item(4)

        for i, j in cross_tiles:
            put(square, (), block(i), block(j), squared(i, j), False)
        for n, (i, j) in enumerate(own_tiles):
            tile = renewed(i, j)
            outgoing[step, n] = tile
            put(signs, (later,), block(i), block(j), tile, i != j)
        trade(step).start()
        for i, j in cross_tiles:
            put(signs, (later,), block(i), block(j), renewed(i, j), True)

    last = (ITERS - 1) % 2
    absorb(ITERS - 2, last)
    far_round(2)
    here = local(a)
    for i in range(BLOCKS):
        high, low = split(dot3(
            signs[last, 0, block(i), :], signs[last, 1, block(i), :],
            signs[last, 0, :, here], signs[last, 1, :, here],
        ))
        latest[0, block(i), :] = high
        latest[1, block(i), :] = low
    for i in range(BLOCKS):
        cubic = dot3(
            signs[last, 0, block(i), :], signs[last, 1, block(i), :], latest[0], latest[1],
        )
        current = signs[last, 0, block(i), here].astype(F32) + signs[last, 1, block(i), here].astype(F32)
        high, low = split(1.5 * current - 0.5 * cubic)
        distance = ((i + 2 * k) % 4 + 4 - a) % 4
        row = pl.ds(pl.multiple_of(jnp.where(distance < 2, distance, 5 - distance) * BLOCK, BLOCK), BLOCK)
        proj[0, row, :] = high
        proj[1, row, :] = low

    def at_hand(q, last_too):
        @pl.when(q != a)
        def _():
            for way in (0, 1):
                wait_near(way, q, 1 - way)
                if last_too:
                    wait_far(way, q)

    def scale(r, columns):
        w = weight[r, columns, :]
        w = 0.5 * (w * w)
        return jnp.concatenate([w, w], axis=1)

    blocks = [a, right, left, across]
    inner = BLOCK * 3

    def filtered_pair(r, low, high):
        x = jnp.concatenate(
            [jnp.concatenate([cube[b, r, low, :], cube[b, r, high, :]], axis=0) for b in blocks], axis=1
        )
        x_high, x_low = split(x)
        product = dot3(x_high, x_low, proj[0], proj[1])
        result[r, low, :] = (cube[a, r, low, :] + product[0:HALF]) * scale(r, low)
        result[r, high, :] = (cube[a, r, high, :] + product[HALF:]) * scale(r, high)

    def begun(q):
        for r in range(ROWS):
            high, low = split(jnp.concatenate([cube[b, r, block(q), :] for b in blocks[:3]], axis=1))
            product = dot3(high, low, proj[0, 0:inner, :], proj[1, 0:inner, :])
            result[r, block(q), :] = cube[a, r, block(q), :] + product

    def finished(q):
        for r in range(ROWS):
            high, low = split(cube[across, r, block(q), :])
            product = dot3(high, low, proj[0, inner:, :], proj[1, inner:, :])
            result[r, block(q), :] = (result[r, block(q), :] + product) * scale(r, block(q))

    def to_hbm(n, r, start, width):
        there = (r, pl.ds(start, width), slice(None))
        return pltpu.make_async_copy(result.at[there], out.at[(0,) + there], out_sem.at[n])

    low_rim = slice(0, OV)
    high_rim = slice(COLS - OV, COLS)
    down = [
        remote(result.at[r, low_rim, :], border.at[1, r], send_border.at[0, r], recv_border.at[0, r], facet_down)
        for r in range(ROWS)
    ]
    up = [
        remote(result.at[r, high_rim, :], border.at[0, r], send_border.at[1, r], recv_border.at[1, r], facet_up)
        for r in range(ROWS)
    ]
    at_hand(0, True)
    at_hand(3, True)
    for r in range(ROWS):
        filtered_pair(r, low_rim, high_rim)

        @pl.when(f > 0)
        def _():
            down[r].start()

        @pl.when(f < 3)
        def _():
            up[r].start()

    for r in range(ROWS):
        filtered_pair(r, slice(OV, BLOCK), slice(COLS - BLOCK, COLS - OV))
    at_hand(1, False)
    at_hand(2, False)
    begun(1)
    begun(2)
    for q in (1, 2):
        @pl.when(q != a)
        def _():
            for way in (0, 1):
                wait_far(way, q)

        finished(q)

    writes = []
    for r in range(ROWS):
        writes.append(to_hbm(len(writes), r, OV, COLS - 2 * OV))
        writes[-1].start()
    for r in range(ROWS):
        @pl.when(f > 0)
        def _():
            down[r].wait_send()
            up[r].wait_recv()
            result[r, low_rim, :] += border[0, r]

        @pl.when(f < 3)
        def _():
            up[r].wait_send()
            down[r].wait_recv()
            result[r, high_rim, :] += border[1, r]

        for start in (0, COLS - OV):
            writes.append(to_hbm(len(writes), r, start, OV))
            writes[-1].start()

    for way in (0, 1):
        for q in range(BLOCKS):
            for h in (0, 1):
                near(way, q, h).wait_send()
            far(way, q).wait_send()
    for d in (1, 2, 3):
        gather_x(d).wait_send()
    for way in (0, 1):
        for e in (0, 1):
            first(e, way).wait_send()
            for h in (0, 1):
                second(e, way, h).wait_send()
    along(low_half(z), 0, at_z(z_up)).wait_send()
    along(high_half(z), 1, at_z(z_up)).wait_send()
    along(low_half(z_down), 2, at_z(z_up)).wait_send()
    along(high_half(z), 3, at_z(z_down)).wait_send()
    along(low_half(z), 4, at_z(z_down)).wait_send()
    along(high_half(z_up), 5, at_z(z_down)).wait_send()
    for step in range(ITERS - 1):
        trade(step).wait_send()
    for slot, zz in enumerate((z, z_down, z_up, z_across)):
        to_mate(whole(zz), slot).wait_send()
    for write in writes:
        write.wait()


def body(facets, profiles, profile_index):
    dma = pltpu.SemaphoreType.DMA
    scratch = [
        pltpu.VMEM((BLOCKS, ROWS, COLS, BLOCK), F32),
        pltpu.VMEM((ROWS, COLS, 128), F32),
        pltpu.VMEM((2, PIXELS, CHANNELS), BF16),
        pltpu.VMEM((2, CHANNELS, PIXELS), BF16),
        pltpu.VMEM((TILES, BLOCK, BLOCK), F32),
        pltpu.VMEM((TILES, BLOCK, BLOCK), F32),
        pltpu.VMEM((TILES, 128, BLOCK), F32),
        pltpu.VMEM((2, TILES, 16, BLOCK), F32),
        pltpu.VMEM((2, 2, TILES, 16, BLOCK), F32),
        pltpu.VMEM((3, TILES, 8, BLOCK), F32),
        pltpu.VMEM((2, 2, CHANNELS, CHANNELS), BF16),
        pltpu.VMEM((2, 2 * BLOCK, CHANNELS), BF16),
        pltpu.VMEM((2, CHANNELS, BLOCK), BF16),
        pltpu.VMEM((2, CHANNELS, BLOCK), BF16),
        pltpu.VMEM((ROWS, COLS, BLOCK), F32),
        pltpu.VMEM((2, ROWS, OV, BLOCK), F32),
        pltpu.VMEM((ITERS - 1, 3, BLOCK, BLOCK), F32),
        pltpu.VMEM((ITERS - 1, 3, BLOCK, BLOCK), F32),
        dma((2, 4, 2)), dma((2, 4, 2)), dma((2, 4)), dma((2, 4)), dma,
        dma((2,)), dma((2,)), dma((2, 2, 3)), dma((2, 2, 3)), dma((3,)), dma((3,)),
        dma((3,)), dma((3,)), dma((6,)), dma((6,)), dma((4,)), dma((4,)),
        dma((2, ROWS)), dma((2, ROWS)), dma((3 * ROWS,)), dma((ITERS - 1,)), dma((ITERS - 1,)),
    ]
    return pl.pallas_call(
        kernel,
        out_shape=jax.ShapeDtypeStruct(facets.shape, F32),
        in_specs=[
            pl.BlockSpec(memory_space=pl.ANY),
            pl.BlockSpec(memory_space=pltpu.VMEM),
            pl.BlockSpec(memory_space=pltpu.SMEM),
        ],
        out_specs=pl.BlockSpec(memory_space=pl.ANY),
        scratch_shapes=scratch,
        compiler_params=pltpu.CompilerParams(
            collective_id=0, has_side_effects=True, vmem_limit_bytes=60 * 2**20
        ),
        cost_estimate=pl.CostEstimate(flops=60 * 10**9, bytes_accessed=6 * 2**20, transcendentals=0),
        name="facet_filter",
    )(facets, profiles, profile_index)


def solution(mesh):
    return jax.shard_map(
        body,
        mesh=mesh,
        in_specs=(P("facet", "pix", None, "chan"), P(), P("facet", "pix")),
        out_specs=P("facet", "pix", None, "chan"),
        check_vma=False,
    )
```

```python
import functools

import jax
import jax.numpy as jnp
from jax import lax
from jax.experimental import pallas as pl
from jax.experimental.pallas import tpu as pltpu
from jax.sharding import PartitionSpec as P

OV = 128
ITERS = 4
EPSILON = 1e-06
MESH = pl.DeviceIdType.MESH
BF16 = jnp.bfloat16
F32 = jnp.float32

ROWS = 3
COLS = 1024
BLOCK = 256
HALF = 128
BLOCKS = 4
CHANNELS = BLOCK * BLOCKS
PIXELS = ROWS * BLOCK
STRIPS = 4
PAIRS = [(0, 0), (1, 1), (2, 2), (3, 3), (0, 1), (1, 2), (2, 3), (3, 0), (0, 2), (1, 3)]
TILES = len(PAIRS)


def dot(a, b):
    return lax.dot_general(a, b, (((1,), (0,)), ((), ())), preferred_element_type=F32)


def dot3(a_high, a_low, b_high, b_low):
    return dot(a_high, b_high) + dot(a_high, b_low) + dot(a_low, b_high)


def split(value):
    high = value.astype(BF16)
    low = (value - high.astype(F32)).astype(BF16)
    return high, low


def block(i):
    return slice(i * BLOCK, (i + 1) * BLOCK)


def kernel(
    facets, profiles, index, out,
    cube, weight, pix_hl, pix_t_hl, gram, total, from_core, from_z1, from_z2, from_x,
    signs, square, latest, proj, result, border, outgoing, incoming,
    send_near, recv_near, send_far, recv_far, own_sem,
    send_core, recv_core, send_z, recv_z, send_x, recv_x,
    send_xg, recv_xg, send_zg, recv_zg, send_cg, recv_cg,
    send_border, recv_border, out_sem, send_tiles, recv_tiles,
):
    f = lax.axis_index("facet")
    p = lax.axis_index("pix")
    a = lax.axis_index("chan")
    z = p // 2
    k = p % 2
    right = (a + 1) % 4
    left = (a + 3) % 4
    across = (a + 2) % 4
    z_up = (z + 1) % 4
    z_down = (z + 3) % 4
    z_across = (z + 2) % 4

    def at_x(chan):
        return (f, p, chan)

    def at_z(zz):
        return (f, zz * 2 + k, a)

    core_mate = (f, z * 2 + (1 - k), a)
    facet_up = ((f + 1) % 4, p, a)
    facet_down = ((f + 3) % 4, p, a)

    barrier = pltpu.get_barrier_semaphore()
    partners = [
        at_x(right), at_x(left), at_x(across), at_z(z_up), at_z(z_down), core_mate, facet_up, facet_down,
    ]
    for partner in partners:
        pl.semaphore_signal(barrier, inc=1, device_id=partner, device_id_type=MESH)
    pl.semaphore_wait(barrier, len(partners))

    def remote(src, dst, send_sem, recv_sem, device):
        return pltpu.make_async_remote_copy(
            src_ref=src, dst_ref=dst, send_sem=send_sem, recv_sem=recv_sem,
            device_id=device, device_id_type=MESH,
        )

    toward = [right, left]
    behind = [left, right]

    def piece(q, h):
        return pl.ds(pl.multiple_of(q * BLOCK + h * HALF, HALF), HALF)

    def near(way, q, h):
        there = cube.at[a, :, piece(q, h), :]
        return remote(
            facets.at[0, :, piece(q, h), :], there,
            send_near.at[way, q, h], recv_near.at[way, q, h], at_x(toward[way]),
        )

    def far(way, q):
        there = cube.at[behind[way], :, piece(q, way), :]
        return remote(there, there, send_far.at[way, q], recv_far.at[way, q], at_x(toward[way]))

    def wait_near(way, q, h):
        there = cube.at[behind[way], :, piece(q, h), :]
        remote(
            there, there, send_near.at[way, q, h], recv_near.at[way, q, h], at_x(toward[way])
        ).wait_recv()

    def wait_far(way, q):
        there = cube.at[across, :, piece(q, way), :]
        remote(there, there, send_far.at[way, q], recv_far.at[way, q], at_x(toward[way])).wait_recv()

    def place(way, q):
        return (4 - q) % 4 if way == 0 else (q + 1) % 4

    def quarter(way, step):
        n = step + jnp.where(place(way, toward[way]) <= step, 1, 0)
        return (4 - n) % 4 if way == 0 else (3 + n) % 4

    def near_item(item, strips=(0, STRIPS)):
        for way in (0, 1):
            n = place(way, across)
            skipped = 2 * (n - jnp.where(place(way, toward[way]) <= n, 1, 0))
            m = item + jnp.where(skipped <= item, 1, 0)
            h = m % 2 if way == 0 else 1 - m % 2
            q = quarter(way, m // 2)
            width = HALF // STRIPS
            strip = pl.ds(
                pl.multiple_of(q * BLOCK + h * HALF + strips[0] * width, width), (strips[1] - strips[0]) * width
            )
            remote(
                facets.at[0, :, strip, :], cube.at[a, :, strip, :],
                send_near.at[way, q, h], recv_near.at[way, q, h], at_x(toward[way]),
            ).start()

    def far_round(step):
        for way in (0, 1):
            q = quarter(way, step)

            @pl.when(q != a)
            def _():
                wait_near(way, q, way)

            far(way, q).start()

    for h in (0, 1):
        for way in (0, 1):
            near(way, toward[way], h).start()
    for way in (0, 1):
        near(way, across, way).start()
    own = pltpu.make_async_copy(facets.at[0], cube.at[a], own_sem)
    own.start()

    for r in range(ROWS):
        row = profiles[0:1, :]
        for n in range(1, profiles.shape[0]):
            row = jnp.where(index[0, r] == n, profiles[n : n + 1, :], row)
        weight[r] = jnp.broadcast_to(row, (128, COLS)).T

    own.wait()

    mine = pl.ds(pl.multiple_of(a * BLOCK, BLOCK), BLOCK)

    def spectra(b, distance):
        for r in range(ROWS):
            w = weight[r, mine, :]
            x = cube[b, r, mine, :] * jnp.concatenate([w, w], axis=1)
            high, low = split(x)
            pix_hl[0, block(r), block(distance)] = high
            pix_hl[1, block(r), block(distance)] = low
            high, low = split(x.T)
            pix_t_hl[0, block(distance), block(r)] = high
            pix_t_hl[1, block(distance), block(r)] = low

    def gram_tile(slot, i, j):
        gram[slot] = dot3(pix_t_hl[0, i, :], pix_t_hl[1, i, :], pix_hl[0, :, j], pix_hl[1, :, j])

    def distant(d):
        return pl.ds(pl.multiple_of(d * BLOCK, BLOCK), BLOCK)

    SPANS = [pl.ds(0, 6), pl.ds(6, 4)]

    def rows(start, count):
        return pl.ds(pl.multiple_of(start, 8), count)

    half = k * 128

    def part(zz):
        return half + zz * 32

    def swap(e):
        return remote(
            gram.at[SPANS[e], rows((1 - k) * 128, 128), :], from_core.at[SPANS[e]],
            send_core.at[e], recv_core.at[e], core_mate,
        )

    def sixteen(e, zz, h):
        return gram.at[SPANS[e], rows(part(zz) + 16 * h, 16), :]

    z_to = [z_up, z_down]

    def first(e, way):
        return remote(
            sixteen(e, z_across, way), from_z1.at[way, SPANS[e]],
            send_z.at[e, way, 0], recv_z.at[e, way, 0], at_z(z_to[way]),
        )

    def second(e, way, h):
        return remote(
            sixteen(e, z_to[way], h), from_z2.at[way, h, SPANS[e]],
            send_z.at[e, way, 1 + h], recv_z.at[e, way, 1 + h], at_z(z_to[way]),
        )

    def cores_summed(e):
        swap(e).start()
        swap(e).wait()
        gram[SPANS[e], rows(half, 128), :] += from_core[SPANS[e]]
        for way in (0, 1):
            first(e, way).start()
        for way in (0, 1):
            second(e, way, 1 - way).start()

    def z_forwarded(e):
        for way in (0, 1):
            first(e, way).wait_recv()
            gram[SPANS[e], rows(part(z_to[way]) + 16 * way, 16), :] += from_z1[way, SPANS[e]]
            second(e, way, way).start()

    def z_summed(e):
        for h in (0, 1):
            second(e, 0, h).wait_recv()
            second(e, 1, h).wait_recv()
            gram[SPANS[e], rows(part(z) + 16 * h, 16), :] += from_z2[0, h, SPANS[e]] + from_z2[1, h, SPANS[e]]

    spectra(a, 0)
    gram_tile(1, block(0), block(0))
    for way in (0, 1):
        wait_near(way, a, 0)
        wait_near(way, a, 1)
    spectra(left, 3)
    spectra(right, 1)
    gram_tile(0, block(3), block(3))
    gram_tile(2, block(1), block(1))
    gram_tile(3, block(3), block(0))
    gram_tile(4, block(0), block(1))
    side = jnp.where((a == 0) | (a == 3), 1, 3)
    gram_tile(5, distant(side), distant(4 - side))
    cores_summed(0)
    for way in (0, 1):
        wait_near(way, toward[way], way)
        far(way, toward[way]).start()
    near_item(0)
    z_forwarded(0)
    for way in (0, 1):
        wait_far(way, a)
    spectra(across, 2)
    gram_tile(6, block(2), block(2))
    gram_tile(7, block(1), block(2))
    gram_tile(8, block(2), block(3))
    side = jnp.where(a < 2, 0, 2)
    gram_tile(9, distant(side), distant(2 - side))
    cores_summed(1)
    near_item(1, (0, 2))
    z_summed(0)
    z_forwarded(1)
    z_summed(1)
    base = part(z)

    scatter = []
    for d in (1, 2, 3):
        target = (a + d) % 4
        scatter.append(remote(
            gram.at[:, rows(base + target * 8, 8), :], from_x.at[d - 1],
            send_x.at[d - 1], recv_x.at[d - 1], at_x(target),
        ))
    for copy in scatter:
        copy.start()
    near_item(1, (2, 3))
    for copy in scatter:
        copy.wait()
    own_rows = rows(base + a * 8, 8)

    def pick(n, values):
        result = values[0]
        for m in range(1, len(values)):
            result = jnp.where(n == m, values[m], result)
        return result

    def slot(chan, t):
        if t < 4:
            return pick((t + 4 - chan) % 4, [1, 2, 6, 0])
        if t < 8:
            return pick((t - chan) % 4, [4, 7, 8, 3])
        return pick((t + chan) % 2, [9, 5])

    for t in range(TILES):
        total[t, own_rows, :] = (
            gram[slot(a, t), own_rows, :] + from_x[0, slot(left, t)]
        ) + (from_x[1, slot(across, t)] + from_x[2, slot(right, t)])

    def gather_x(d):
        return remote(
            total.at[:, own_rows, :], total.at[:, own_rows, :],
            send_xg.at[d - 1], recv_xg.at[d - 1], at_x((a + d) % 4),
        )

    for d in (1, 2, 3):
        gather_x(d).start()
    near_item(1, (3, 4))
    far_round(0)
    near_item(2)
    near_item(3)
    for d in (1, 2, 3):
        there = total.at[:, rows(base + ((a + 4 - d) % 4) * 8, 8), :]
        remote(there, there, send_xg.at[d - 1], recv_xg.at[d - 1], at_x((a + d) % 4)).wait_recv()

    def whole(zz):
        return total.at[:, rows(part(zz), 32), :]

    def low_half(zz):
        return total.at[:, rows(part(zz), 16), :]

    def high_half(zz):
        return total.at[:, rows(part(zz) + 16, 16), :]

    def along(ref, slot, device):
        return remote(ref, ref, send_zg.at[slot], recv_zg.at[slot], device)

    def to_mate(ref, slot):
        return remote(ref, ref, send_cg.at[slot], recv_cg.at[slot], core_mate)

    along(low_half(z), 0, at_z(z_up)).start()
    along(high_half(z), 3, at_z(z_down)).start()
    along(high_half(z), 1, at_z(z_up)).start()
    along(low_half(z), 4, at_z(z_down)).start()
    to_mate(whole(z), 0).start()
    along(low_half(z_down), 0, at_z(z_up)).wait_recv()
    along(low_half(z_down), 2, at_z(z_up)).start()
    along(high_half(z_up), 3, at_z(z_down)).wait_recv()
    along(high_half(z_up), 5, at_z(z_down)).start()
    along(high_half(z_down), 1, at_z(z_up)).wait_recv()
    to_mate(whole(z_down), 1).start()
    along(low_half(z_up), 4, at_z(z_down)).wait_recv()
    to_mate(whole(z_up), 2).start()
    along(low_half(z_across), 2, at_z(z_up)).wait_recv()
    along(high_half(z_across), 5, at_z(z_down)).wait_recv()
    to_mate(whole(z_across), 3).start()

    def mate_whole(zz):
        return total.at[:, rows((1 - k) * 128 + zz * 32, 32), :]

    for slot, zz in enumerate((z, z_down, z_up, z_across)):
        to_mate(mate_whole(zz), slot).wait_recv()

    eye = (
        lax.broadcasted_iota(jnp.int32, (BLOCK, BLOCK), 0) == lax.broadcasted_iota(jnp.int32, (BLOCK, BLOCK), 1)
    ).astype(F32)

    def add_up(tile):
        return jnp.sum(jnp.sum(tile, axis=0, keepdims=True), axis=1, keepdims=True)

    diagonal = total[0] * eye
    for t in range(1, BLOCKS):
        diagonal = diagonal + total[t] * eye
    mean_eig = add_up(diagonal) / CHANNELS
    squares = None
    for t in range(TILES):
        if t < BLOCKS:
            moved = total[t] - mean_eig * eye
            term = moved * moved
        else:
            term = 2.0 * (total[t] * total[t])
        squares = term if squares is None else squares + term
    spread = jnp.sqrt(add_up(squares) + EPSILON)

    def put(ref, lead, i, j, tile, mirror):
        high, low = split(tile)
        ref[lead + (0, i, j)] = high
        ref[lead + (1, i, j)] = low
        if mirror:
            high, low = split(tile.T)
            ref[lead + (0, j, i)] = high
            ref[lead + (1, j, i)] = low

    def local(b):
        return pl.ds(pl.multiple_of(((b + 2 * k) % 4) * BLOCK, BLOCK), BLOCK)

    for t, (i, j) in enumerate(PAIRS):
        tile = total[t]
        if i == j:
            tile = tile - mean_eig * eye
        put(signs, (0,), local(i), local(j), tile / spread, i != j)

    own_tiles = [(0, 0), (0, 1), (1, 1)]
    cross_tiles = [(0, 2), (0, 3), (1, 2), (1, 3)]

    def trade(step):
        return remote(outgoing.at[step], incoming.at[step], send_tiles.at[step], recv_tiles.at[step], core_mate)

    def absorb(step, buffer):
        trade(step).wait_recv()
        for n, (i, j) in enumerate(own_tiles):
            put(signs, (buffer,), block(i + 2), block(j + 2), incoming[step, n], i != j)

    for step in range(ITERS - 1):
        now = step % 2
        later = 1 - now

        def squared(i, j):
            return dot3(
                signs[now, 0, block(i), :], signs[now, 1, block(i), :],
                signs[now, 0, :, block(j)], signs[now, 1, :, block(j)],
            )

        def renewed(i, j):
            cubic = dot3(
                square[0, block(i), :], square[1, block(i), :],
                signs[now, 0, :, block(j)], signs[now, 1, :, block(j)],
            )
            current = signs[now, 0, block(i), block(j)].astype(F32) + signs[now, 1, block(i), block(j)].astype(F32)
            return 1.5 * current - 0.5 * cubic

        for i, j in own_tiles:
            put(square, (), block(i), block(j), squared(i, j), i != j)

        if step > 0:
            absorb(step - 1, now)
        if step == 1:
            far_round(1)
            near_item(4)
        if step == 2:
            far_round(2)

        for i, j in cross_tiles:
            put(square, (), block(i), block(j), squared(i, j), False)
        for n, (i, j) in enumerate(own_tiles):
            tile = renewed(i, j)
            outgoing[step, n] = tile
            put(signs, (later,), block(i), block(j), tile, i != j)
        trade(step).start()
        for i, j in cross_tiles:
            put(signs, (later,), block(i), block(j), renewed(i, j), True)

    last = (ITERS - 1) % 2
    absorb(ITERS - 2, last)
    here = local(a)
    for i in range(BLOCKS):
        high, low = split(dot3(
            signs[last, 0, block(i), :], signs[last, 1, block(i), :],
            signs[last, 0, :, here], signs[last, 1, :, here],
        ))
        latest[0, block(i), :] = high
        latest[1, block(i), :] = low
    for i in range(BLOCKS):
        cubic = dot3(
            signs[last, 0, block(i), :], signs[last, 1, block(i), :], latest[0], latest[1],
        )
        current = signs[last, 0, block(i), here].astype(F32) + signs[last, 1, block(i), here].astype(F32)
        high, low = split(1.5 * current - 0.5 * cubic)
        distance = ((i + 2 * k) % 4 + 4 - a) % 4
        row = pl.ds(pl.multiple_of(jnp.where(distance < 2, distance, 5 - distance) * BLOCK, BLOCK), BLOCK)
        proj[0, row, :] = high
        proj[1, row, :] = low

    def at_hand(q, last_too):
        @pl.when(q != a)
        def _():
            for way in (0, 1):
                wait_near(way, q, 1 - way)
                if last_too:
                    wait_far(way, q)

    def scale(r, columns):
        w = weight[r, columns, :]
        w = 0.5 * (w * w)
        return jnp.concatenate([w, w], axis=1)

    blocks = [a, right, left, across]
    inner = BLOCK * 3

    def filtered_pair(r, low, high):
        x = jnp.concatenate(
            [jnp.concatenate([cube[b, r, low, :], cube[b, r, high, :]], axis=0) for b in blocks], axis=1
        )
        x_high, x_low = split(x)
        product = dot3(x_high, x_low, proj[0], proj[1])
        result[r, low, :] = (cube[a, r, low, :] + product[0:HALF]) * scale(r, low)
        result[r, high, :] = (cube[a, r, high, :] + product[HALF:]) * scale(r, high)

    def begun(q):
        for r in range(ROWS):
            high, low = split(jnp.concatenate([cube[b, r, block(q), :] for b in blocks[:3]], axis=1))
            product = dot3(high, low, proj[0, 0:inner, :], proj[1, 0:inner, :])
            result[r, block(q), :] = cube[a, r, block(q), :] + product

    def finished(q):
        for r in range(ROWS):
            high, low = split(cube[across, r, block(q), :])
            product = dot3(high, low, proj[0, inner:, :], proj[1, inner:, :])
            result[r, block(q), :] = (result[r, block(q), :] + product) * scale(r, block(q))

    def to_hbm(n, r, start, width):
        there = (r, pl.ds(start, width), slice(None))
        return pltpu.make_async_copy(result.at[there], out.at[(0,) + there], out_sem.at[n])

    low_rim = slice(0, OV)
    high_rim = slice(COLS - OV, COLS)
    down = [
        remote(result.at[r, low_rim, :], border.at[1, r], send_border.at[0, r], recv_border.at[0, r], facet_down)
        for r in range(ROWS)
    ]
    up = [
        remote(result.at[r, high_rim, :], border.at[0, r], send_border.at[1, r], recv_border.at[1, r], facet_up)
        for r in range(ROWS)
    ]
    writes = []

    def write_out(r, start, width):
        writes.append(to_hbm(len(writes), r, start, width))
        writes[-1].start()

    at_hand(0, True)
    at_hand(3, True)
    for r in range(ROWS):
        filtered_pair(r, low_rim, high_rim)

        @pl.when(f > 0)
        def _():
            down[r].start()

        @pl.when(f < 3)
        def _():
            up[r].start()

    for r in range(ROWS):
        filtered_pair(r, slice(OV, BLOCK), slice(COLS - BLOCK, COLS - OV))
        for start in (OV, COLS - BLOCK):
            write_out(r, start, HALF)
    at_hand(1, False)
    at_hand(2, False)
    begun(1)
    begun(2)
    for q in (1, 2):
        @pl.when(q != a)
        def _():
            for way in (0, 1):
                wait_far(way, q)

        finished(q)
        for r in range(ROWS):
            write_out(r, q * BLOCK, BLOCK)

    for r in range(ROWS):
        @pl.when(f > 0)
        def _():
            down[r].wait_send()
            up[r].wait_recv()
            result[r, low_rim, :] += border[0, r]

        @pl.when(f < 3)
        def _():
            up[r].wait_send()
            down[r].wait_recv()
            result[r, high_rim, :] += border[1, r]

        for start in (0, COLS - OV):
            write_out(r, start, OV)

    for way in (0, 1):
        for q in range(BLOCKS):
            for h in (0, 1):
                near(way, q, h).wait_send()
            far(way, q).wait_send()
    for d in (1, 2, 3):
        gather_x(d).wait_send()
    for way in (0, 1):
        for e in (0, 1):
            first(e, way).wait_send()
            for h in (0, 1):
                second(e, way, h).wait_send()
    along(low_half(z), 0, at_z(z_up)).wait_send()
    along(high_half(z), 1, at_z(z_up)).wait_send()
    along(low_half(z_down), 2, at_z(z_up)).wait_send()
    along(high_half(z), 3, at_z(z_down)).wait_send()
    along(low_half(z), 4, at_z(z_down)).wait_send()
    along(high_half(z_up), 5, at_z(z_down)).wait_send()
    for step in range(ITERS - 1):
        trade(step).wait_send()
    for slot, zz in enumerate((z, z_down, z_up, z_across)):
        to_mate(whole(zz), slot).wait_send()
    for write in writes:
        write.wait()


def body(facets, profiles, profile_index):
    dma = pltpu.SemaphoreType.DMA
    scratch = [
        pltpu.VMEM((BLOCKS, ROWS, COLS, BLOCK), F32),
        pltpu.VMEM((ROWS, COLS, 128), F32),
        pltpu.VMEM((2, PIXELS, CHANNELS), BF16),
        pltpu.VMEM((2, CHANNELS, PIXELS), BF16),
        pltpu.VMEM((TILES, BLOCK, BLOCK), F32),
        pltpu.VMEM((TILES, BLOCK, BLOCK), F32),
        pltpu.VMEM((TILES, 128, BLOCK), F32),
        pltpu.VMEM((2, TILES, 16, BLOCK), F32),
        pltpu.VMEM((2, 2, TILES, 16, BLOCK), F32),
        pltpu.VMEM((3, TILES, 8, BLOCK), F32),
        pltpu.VMEM((2, 2, CHANNELS, CHANNELS), BF16),
        pltpu.VMEM((2, 2 * BLOCK, CHANNELS), BF16),
        pltpu.VMEM((2, CHANNELS, BLOCK), BF16),
        pltpu.VMEM((2, CHANNELS, BLOCK), BF16),
        pltpu.VMEM((ROWS, COLS, BLOCK), F32),
        pltpu.VMEM((2, ROWS, OV, BLOCK), F32),
        pltpu.VMEM((ITERS - 1, 3, BLOCK, BLOCK), F32),
        pltpu.VMEM((ITERS - 1, 3, BLOCK, BLOCK), F32),
        dma((2, 4, 2)), dma((2, 4, 2)), dma((2, 4)), dma((2, 4)), dma,
        dma((2,)), dma((2,)), dma((2, 2, 3)), dma((2, 2, 3)), dma((3,)), dma((3,)),
        dma((3,)), dma((3,)), dma((6,)), dma((6,)), dma((4,)), dma((4,)),
        dma((2, ROWS)), dma((2, ROWS)), dma((6 * ROWS,)), dma((ITERS - 1,)), dma((ITERS - 1,)),
    ]
    return pl.pallas_call(
        kernel,
        out_shape=jax.ShapeDtypeStruct(facets.shape, F32),
        in_specs=[
            pl.BlockSpec(memory_space=pl.ANY),
            pl.BlockSpec(memory_space=pltpu.VMEM),
            pl.BlockSpec(memory_space=pltpu.SMEM),
        ],
        out_specs=pl.BlockSpec(memory_space=pl.ANY),
        scratch_shapes=scratch,
        compiler_params=pltpu.CompilerParams(
            collective_id=0, has_side_effects=True, vmem_limit_bytes=60 * 2**20
        ),
        cost_estimate=pl.CostEstimate(flops=60 * 10**9, bytes_accessed=6 * 2**20, transcendentals=0),
        name="facet_filter",
    )(facets, profiles, profile_index)


def solution(mesh):
    return jax.shard_map(
        body,
        mesh=mesh,
        in_specs=(P("facet", "pix", None, "chan"), P(), P("facet", "pix")),
        out_specs=P("facet", "pix", None, "chan"),
        check_vma=False,
    )
```
